32 devices in a mesh: groups: 2 (over x), outd: 8 (over z, y), ind: 2 (over core).
Axes of the slice: x: 2, y: 2, z: 4, core: 2. Of those that a mesh axis runs over, the one named last changes fastest.
Arguments:
- activations: bfloat16 [1024, 5120], P(('groups', 'outd'), 'ind'), parts along dimension 0, may hold values from -6 to 6
- out_grads: bfloat16 [1024, 27648], P(('groups', 'ind'), 'outd'), parts along dimension 0, may hold values from -6 to 6
- query_grads: bfloat16 [4, 5120, 27648], P(None, 'ind', 'outd'), may hold values from -0.0014953613 to 0.0014953613
Outputs:
- scores: float32 [4, 1024], P(None, ('groups', 'outd', 'ind')), parts along dimension 1
The draws below stay inside these ranges and needn't reach their ends.
There are 2 independent parts, one for each index of `groups`. The reference program is written for one: setup_inputs(seed, part) draws one part's arguments, and reference() takes and returns one part's arrays. A program takes and returns all parts, laid end to end along the dimension named above; an argument that names none is the same for every part. Nothing has to cross between parts.
All inputs are finite; a program needn't handle non-finite values.
Results may differ from the reference program's by a relative error of at most 0.0003.
Values may be sent and summed in bfloat16 or wider, within the bound.
A program may use at most 192 MiB of HBM per device.

```python
import jax
import jax.numpy as jnp
from jax import lax

D_IN = 5120
D_OUT = 27648
QUERIES = 4
TOKENS = 512


def steps_of(key, dims, pieces, least, top_value):
    gain, own = 1.0, jax.random.fold_in(key, 6)
    for dim, shards_of in pieces:
        steps = jnp.exp(jax.random.uniform(jax.random.fold_in(own, dim), (shards_of,), jnp.float32, least / len(pieces), top_value / len(pieces)))
        gain = gain * jnp.repeat(steps, dims[dim] // shards_of).reshape([-1 if axis == dim else 1 for axis in range(len(dims))])
    return gain


def normal_values(key, dims, width, bound, cuts=(), dtype=jnp.bfloat16):
    array = width * jax.random.normal(key, dims, jnp.float32)
    if cuts:
        array = array * steps_of(key, dims, cuts, -0.22, 0.18)
    return jnp.clip(array, -bound, bound).astype(dtype)


def setup_inputs(seed: int = 0, part: int = 0) -> dict:
    arg_keys = jax.random.split(jax.random.key(seed), 4)
    own_keys = jax.random.split(jax.random.fold_in(arg_keys[3], part), 4)
    activations = normal_values(own_keys[0], (TOKENS, D_IN), 1.0, 6.0, ((0, 8), (1, 2)))
    out_grads = normal_values(own_keys[1], (TOKENS, D_OUT), 1.0, 6.0, ((0, 2), (1, 8)))
    query_grads = normal_values(arg_keys[2], (QUERIES, D_IN, D_OUT), 0.00025, 0.0014953613, ((1, 2), (2, 8)))
    return dict(activations=activations, out_grads=out_grads, query_grads=query_grads)


def reference(activations, out_grads, query_grads):
    grads_wide = out_grads.astype(jnp.float32)

    def one_query(query_tile):
        projected = jnp.dot(activations, query_tile, preferred_element_type=jnp.float32)
        return jnp.sum(projected * grads_wide, axis=1)

    return lax.map(one_query, query_grads)
```

```python
import functools

import jax
import jax.numpy as jnp
from jax import lax
from jax.experimental import pallas as pl
from jax.experimental.pallas import tpu as pltpu
from jax.sharding import PartitionSpec as P

MESH = pl.DeviceIdType.MESH
ROWS = 256
PLANE = 2


def kernel(n_out, n_in, a_hbm, g_hbm, q_hbm, out_ref,
           a_all, g_all, w_buf, held, acc, part, inbox,
           w_sem, own_sem, g_sem, a_send, a_recv, s_send, s_recv):
    queries, width, cols = q_hbm.shape
    block_t = a_hbm.shape[0]
    half_t = g_hbm.shape[0]
    tokens = block_t * n_out
    steps = width // ROWS
    line_len = n_out // PLANE
    total = n_out * n_in
    mo, mi = lax.axis_index("outd"), lax.axis_index("ind")
    line, plane = mo // PLANE, mo % PLANE
    me = mo * n_in + mi

    def fetch(s, slot):
        return pltpu.make_async_copy(
            q_hbm.at[:, pl.ds(s * ROWS, ROWS), :], w_buf.at[slot], w_sem.at[slot])

    own_g = pltpu.make_async_copy(g_hbm, g_all.at[mi], own_sem.at[0])
    own_a = pltpu.make_async_copy(a_hbm, a_all.at[mo], own_sem.at[1])
    own_g.start()
    fetch(0, 0).start()
    own_a.start()

    barrier = pltpu.get_barrier_semaphore()
    for k in range(1, total):
        peer = lax.rem(me + k, total)
        pl.semaphore_signal(barrier, inc=1, device_id={"outd": peer // n_in, "ind": peer % n_in},
                            device_id_type=MESH)
    pl.semaphore_wait(barrier, total - 1)

    g_copy = pltpu.make_async_remote_copy(
        src_ref=g_hbm, dst_ref=g_all.at[mi], send_sem=g_sem.at[0], recv_sem=g_sem.at[1],
        device_id={"ind": 1 - mi}, device_id_type=MESH)
    g_wait = pltpu.make_async_remote_copy(
        src_ref=g_hbm, dst_ref=g_all.at[1 - mi], send_sem=g_sem.at[0], recv_sem=g_sem.at[1],
        device_id={"ind": 1 - mi}, device_id_type=MESH)
    g_copy.start()

    def hop(slot, direction, src=None):
        to = (mo + PLANE, mo - PLANE, line * PLANE + (1 - plane))[direction]
        return pltpu.make_async_remote_copy(
            src_ref=a_all.at[slot] if src is None else src, dst_ref=a_all.at[slot],
            send_sem=a_send.at[direction, slot], recv_sem=a_recv.at[slot],
            device_id={"outd": to}, device_id_type=MESH)

    hop(mo, 2, a_hbm).start()

    @pl.when(line < line_len - 1)
    def _():
        hop(mo, 0, a_hbm).start()

    @pl.when(line > 0)
    def _():
        hop(mo, 1, a_hbm).start()

    def relay(distance):
        low, high = mo - distance * PLANE, mo + distance * PLANE

        @pl.when(line >= distance)
        def _():
            hop(low, 0).wait_recv()

            @pl.when(line < line_len - 1)
            def _():
                hop(low, 0).start()

            hop(low, 2).start()

        @pl.when(line + distance < line_len)
        def _():
            hop(high, 1).wait_recv()

            @pl.when(line > 0)
            def _():
                hop(high, 1).start()

            hop(high, 2).start()

    def dot(w, g):
        return lax.dot_general(w.reshape(queries * ROWS, cols), g, (((1,), (1,)), ((), ())),
                               preferred_element_type=jnp.float32)

    def half(slot, which):
        at = pl.multiple_of(which * half_t, 128)
        held[0, :, pl.ds(at, half_t)] = dot(w_buf[slot], g_all[which])

    fetch(1, 1).start()
    own_g.wait()
    fetch(0, 0).wait()
    half(0, mi)
    g_wait.wait_recv()
    half(0, 1 - mi)

    tail = 2
    waits = {2: 1, 4: 2, 6: 3}

    def step(s, carry):
        slot = lax.rem(s, 2)
        for at, distance in waits.items():
            if distance < line_len:
                @pl.when(s == at)
                def _():
                    relay(distance)
        fetch(s + 1, 1 - slot).start()
        fetch(s, slot).wait()
        held[s] = dot(w_buf[slot], g_all[...].reshape(tokens, cols))
        return carry

    lax.fori_loop(1, steps - tail, step, 0)

    for other in range(line_len):
        hop(other * PLANE + (1 - plane), 2).wait_recv()
    own_a.wait()

    def weigh(s, block):
        a_t = a_all[:, :, s * ROWS:(s + 1) * ROWS].reshape(tokens, ROWS).astype(jnp.float32).T
        return (block.reshape(queries, ROWS // 8, 8, tokens) * a_t.reshape(ROWS // 8, 8, tokens)).sum(1)

    acc[...] = jnp.zeros_like(acc)
    done = 0
    for s in range(steps - tail, steps):
        slot = s % 2
        if s + 1 < steps:
            fetch(s + 1, 1 - slot).start()
        fetch(s, slot).wait()
        upto = s * (s - steps + tail + 1) // tail
        found = acc[...]
        for earlier in range(done, upto):
            found += weigh(earlier, held[earlier])
        done = upto
        held[s] = dot(w_buf[slot], g_all[...].reshape(tokens, cols))
        acc[...] = found
    found = acc[...]
    for earlier in range(done, steps):
        found += weigh(earlier, held[earlier])
    mine = found.sum(1)

    lanes = 128
    share = tokens // total
    per = lanes // share
    for z in range(tokens // lanes):
        part[z, 0:queries] = mine[:, z * lanes:(z + 1) * lanes]
        part[z, queries:8] = jnp.zeros((8 - queries, lanes), jnp.float32)

    def give(k):
        peer = lax.rem(me + k, total)
        return pltpu.make_async_remote_copy(
            src_ref=part.at[peer // per], dst_ref=inbox.at[k], send_sem=s_send.at[k], recv_sem=s_recv.at[k],
            device_id={"outd": peer // n_in, "ind": peer % n_in}, device_id_type=MESH)

    for k in range(1, total):
        give(k).start()

    g_copy.wait_send()
    hop(mo, 2, a_hbm).wait_send()
    for other in range(line_len):
        slot = other * PLANE + plane

        @pl.when(other != line)
        def _():
            hop(slot, 2).wait_send()

        @pl.when(jnp.logical_and(other <= line, line < line_len - 1))
        def _():
            hop(slot, 0).wait_send()

        @pl.when(jnp.logical_and(other >= line, line > 0))
        def _():
            hop(slot, 1).wait_send()

    sums = part[me // per]
    for k in range(1, total):
        give(k).wait_recv()
        sums += inbox[k]
    sums = sums[0:queries]
    place = lax.rem(me, per)
    result = sums[:, 0:share]
    for p in range(1, per):
        result = jnp.where(place == p, sums[:, p * share:(p + 1) * share], result)
    out_ref[...] = result
    for k in range(1, total):
        give(k).wait_send()


def fused(n_out, n_in, activations, out_grads, query_grads):
    queries, width, cols = query_grads.shape
    block_t, half_t = activations.shape[0], out_grads.shape[0]
    tokens, total = block_t * n_out, n_out * n_in
    steps = width // ROWS
    anywhere = pl.BlockSpec(memory_space=pl.ANY)
    dma = pltpu.SemaphoreType.DMA
    return pl.pallas_call(
        functools.partial(kernel, n_out, n_in),
        out_shape=jax.ShapeDtypeStruct((queries, tokens // total), jnp.float32),
        in_specs=[anywhere] * 3,
        out_specs=pl.BlockSpec(memory_space=pltpu.VMEM),
        scratch_shapes=[
            pltpu.VMEM((n_out, block_t, width), jnp.bfloat16),
            pltpu.VMEM((n_in, half_t, cols), jnp.bfloat16),
            pltpu.VMEM((2, queries, ROWS, cols), jnp.bfloat16),
            pltpu.VMEM((steps, queries * ROWS, tokens), jnp.float32),
            pltpu.VMEM((queries, 8, tokens), jnp.float32),
            pltpu.VMEM((tokens // 128, 8, 128), jnp.float32),
            pltpu.VMEM((total, 8, 128), jnp.float32),
            dma((2,)),
            dma((2,)),
            dma((2,)),
            dma((3, n_out)),
            dma((n_out,)),
            dma((total,)),
            dma((total,)),
        ],
        compiler_params=pltpu.CompilerParams(
            collective_id=0, has_side_effects=True, vmem_limit_bytes=60 * 2**20),
        cost_estimate=pl.CostEstimate(
            flops=2 * queries * tokens * width * cols, bytes_accessed=2 * query_grads.size, transcendentals=0),
    )(activations, out_grads, query_grads)


def plain(activations, out_grads, query_grads):
    gradient = lax.all_gather(out_grads, "ind", axis=0, tiled=True)
    gathered = lax.all_gather(activations, "outd", axis=0, tiled=True)
    projected = jnp.einsum("ti,qio->qto", gathered, query_grads, preferred_element_type=jnp.float32)
    partial_sum = jnp.einsum("qto,to->qt", projected, gradient.astype(jnp.float32))
    return lax.psum_scatter(partial_sum, ("outd", "ind"), scatter_dimension=1, tiled=True)


def local(n_out, n_in, activations, out_grads, query_grads):
    queries, width, cols = query_grads.shape
    block_t, half_t = activations.shape[0], out_grads.shape[0]
    tokens, total = block_t * n_out, n_out * n_in
    fits = (n_in == 2 and n_out == 4 * PLANE and queries <= 8 and block_t % 16 == 0 and half_t % 128 == 0
            and cols % 128 == 0 and width % (2 * ROWS) == 0 and width // ROWS >= 8 and tokens % 128 == 0
            and 128 % (tokens // total) == 0
            and (2 * queries * ROWS * cols + tokens * (cols + width)) * 2 + queries * width * tokens * 4 < 56 * 2**20)
    if fits:
        return fused(n_out, n_in, activations, out_grads, query_grads)
    return plain(activations, out_grads, query_grads)


def solution(mesh):
    in_specs = (P(("groups", "outd"), "ind"), P(("groups", "ind"), "outd"), P(None, "ind", "outd"))
    out_specs = P(None, ("groups", "outd", "ind"))
    return jax.shard_map(functools.partial(local, mesh.shape["outd"], mesh.shape["ind"]),
                         mesh=mesh, in_specs=in_specs, out_specs=out_specs, check_vma=False)
```

```python
import functools

import jax
import jax.numpy as jnp
from jax import lax
from jax.experimental import pallas as pl
from jax.experimental.pallas import tpu as pltpu
from jax.sharding import PartitionSpec as P

MESH = pl.DeviceIdType.MESH
ROWS = 256
PLANE = 2


def kernel(n_out, n_in, a_hbm, g_hbm, q_hbm, out_ref,
           a_all, g_all, w_buf, held, acc, part, inbox,
           w_sem, own_sem, g_sem, a_send, a_recv, s_send, s_recv):
    queries, width, cols = q_hbm.shape
    block_t = a_hbm.shape[0]
    half_t = g_hbm.shape[0]
    tokens = block_t * n_out
    steps = width // ROWS
    line_len = n_out // PLANE
    total = n_out * n_in
    mo, mi = lax.axis_index("outd"), lax.axis_index("ind")
    line, plane = mo // PLANE, mo % PLANE
    me = mo * n_in + mi

    def fetch(s, slot):
        return pltpu.make_async_copy(
            q_hbm.at[:, pl.ds(s * ROWS, ROWS), :], w_buf.at[slot], w_sem.at[slot])

    pair = queries // 2

    def first(p):
        at = pl.ds(p * pair, pair)
        return pltpu.make_async_copy(
            q_hbm.at[at, pl.ds(0, ROWS), :], w_buf.at[0, at], w_sem.at[3 * p])

    own_g = pltpu.make_async_copy(g_hbm, g_all.at[mi], own_sem.at[0])
    own_a = pltpu.make_async_copy(a_hbm, a_all.at[mo], own_sem.at[1])
    own_g.start()
    for p in range(2):
        first(p).start()
    own_a.start()

    barrier = pltpu.get_barrier_semaphore()
    for k in range(1, total):
        peer = lax.rem(me + k, total)
        pl.semaphore_signal(barrier, inc=1, device_id={"outd": peer // n_in, "ind": peer % n_in},
                            device_id_type=MESH)
    pl.semaphore_wait(barrier, total - 1)

    g_copy = pltpu.make_async_remote_copy(
        src_ref=g_hbm, dst_ref=g_all.at[mi], send_sem=g_sem.at[0], recv_sem=g_sem.at[1],
        device_id={"ind": 1 - mi}, device_id_type=MESH)
    g_wait = pltpu.make_async_remote_copy(
        src_ref=g_hbm, dst_ref=g_all.at[1 - mi], send_sem=g_sem.at[0], recv_sem=g_sem.at[1],
        device_id={"ind": 1 - mi}, device_id_type=MESH)
    g_copy.start()

    def hop(slot, direction, src=None):
        to = (mo + PLANE, mo - PLANE, line * PLANE + (1 - plane))[direction]
        return pltpu.make_async_remote_copy(
            src_ref=a_all.at[slot] if src is None else src, dst_ref=a_all.at[slot],
            send_sem=a_send.at[direction, slot], recv_sem=a_recv.at[slot],
            device_id={"outd": to}, device_id_type=MESH)

    hop(mo, 2, a_hbm).start()

    @pl.when(line < line_len - 1)
    def _():
        hop(mo, 0, a_hbm).start()

    @pl.when(line > 0)
    def _():
        hop(mo, 1, a_hbm).start()

    def relay(distance):
        low, high = mo - distance * PLANE, mo + distance * PLANE

        @pl.when(line >= distance)
        def _():
            hop(low, 0).wait_recv()

            @pl.when(line < line_len - 1)
            def _():
                hop(low, 0).start()

            hop(low, 2).start()

        @pl.when(line + distance < line_len)
        def _():
            hop(high, 1).wait_recv()

            @pl.when(line > 0)
            def _():
                hop(high, 1).start()

            hop(high, 2).start()

    def dot(w, g):
        return lax.dot_general(w.reshape(w.shape[0] * ROWS, cols), g, (((1,), (1,)), ((), ())),
                               preferred_element_type=jnp.float32)

    def half(s, which):
        at = pl.multiple_of(which * half_t, 128)
        held[s, :, pl.ds(at, half_t)] = dot(w_buf[s], g_all[which])

    own_g.wait()
    at = pl.multiple_of(mi * half_t, 128)
    for p in range(2):
        first(p).wait()
        if p == 1:
            fetch(1, 1).start()
        held[0, p * pair * ROWS:(p + 1) * pair * ROWS, pl.ds(at, half_t)] = dot(
            w_buf[0, p * pair:(p + 1) * pair], g_all[mi])
    fetch(1, 1).wait()
    fetch(2, 2).start()
    half(1, mi)
    g_wait.wait_recv()
    half(0, 1 - mi)
    half(1, 1 - mi)

    tail = 2
    waits = {2: 1, 4: 2, 6: 3}

    def step(s, carry):
        slot = lax.rem(s, 3)
        for at, distance in waits.items():
            if distance < line_len:
                @pl.when(s == at)
                def _():
                    relay(distance)
        fetch(s + 1, lax.rem(s + 1, 3)).start()
        fetch(s, slot).wait()
        held[s] = dot(w_buf[slot], g_all[...].reshape(tokens, cols))
        return carry

    lax.fori_loop(2, steps - tail, step, 0)

    for other in range(line_len):
        hop(other * PLANE + (1 - plane), 2).wait_recv()
    own_a.wait()

    def weigh(s, block):
        a_t = a_all[:, :, s * ROWS:(s + 1) * ROWS].reshape(tokens, ROWS).astype(jnp.float32).T
        return (block.reshape(queries, ROWS // 8, 8, tokens) * a_t.reshape(ROWS // 8, 8, tokens)).sum(1)

    acc[...] = jnp.zeros_like(acc)
    done = 0
    for s in range(steps - tail, steps):
        slot = s % 3
        if s + 1 < steps:
            fetch(s + 1, (s + 1) % 3).start()
        fetch(s, slot).wait()
        upto = s * (s - steps + tail + 1) // tail
        found = acc[...]
        for earlier in range(done, upto):
            found += weigh(earlier, held[earlier])
        done = upto
        held[s] = dot(w_buf[slot], g_all[...].reshape(tokens, cols))
        acc[...] = found
    found = acc[...]
    for earlier in range(done, steps):
        found += weigh(earlier, held[earlier])
    mine = found.sum(1)

    lanes = 128
    share = tokens // total
    per = lanes // share
    for z in range(tokens // lanes):
        part[z, 0:queries] = mine[:, z * lanes:(z + 1) * lanes]
        part[z, queries:8] = jnp.zeros((8 - queries, lanes), jnp.float32)

    def give(k):
        peer = lax.rem(me + k, total)
        return pltpu.make_async_remote_copy(
            src_ref=part.at[peer // per], dst_ref=inbox.at[k], send_sem=s_send.at[k], recv_sem=s_recv.at[k],
            device_id={"outd": peer // n_in, "ind": peer % n_in}, device_id_type=MESH)

    for k in range(1, total):
        give(k).start()

    g_copy.wait_send()
    hop(mo, 2, a_hbm).wait_send()
    for other in range(line_len):
        slot = other * PLANE + plane

        @pl.when(other != line)
        def _():
            hop(slot, 2).wait_send()

        @pl.when(jnp.logical_and(other <= line, line < line_len - 1))
        def _():
            hop(slot, 0).wait_send()

        @pl.when(jnp.logical_and(other >= line, line > 0))
        def _():
            hop(slot, 1).wait_send()

    sums = part[me // per]
    for k in range(1, total):
        give(k).wait_recv()
        sums += inbox[k]
    out_ref[...] = sums
    for k in range(1, total):
        give(k).wait_send()


def fused(n_out, n_in, activations, out_grads, query_grads):
    queries, width, cols = query_grads.shape
    block_t, half_t = activations.shape[0], out_grads.shape[0]
    tokens, total = block_t * n_out, n_out * n_in
    share = tokens // total
    steps = width // ROWS
    anywhere = pl.BlockSpec(memory_space=pl.ANY)
    dma = pltpu.SemaphoreType.DMA
    sums = pl.pallas_call(
        functools.partial(kernel, n_out, n_in),
        out_shape=jax.ShapeDtypeStruct((8, 128), jnp.float32),
        in_specs=[anywhere] * 3,
        out_specs=pl.BlockSpec(memory_space=pltpu.VMEM),
        scratch_shapes=[
            pltpu.VMEM((n_out, block_t, width), jnp.bfloat16),
            pltpu.VMEM((n_in, half_t, cols), jnp.bfloat16),
            pltpu.VMEM((3, queries, ROWS, cols), jnp.bfloat16),
            pltpu.VMEM((steps, queries * ROWS, tokens), jnp.float32),
            pltpu.VMEM((queries, 8, tokens), jnp.float32),
            pltpu.VMEM((tokens // 128, 8, 128), jnp.float32),
            pltpu.VMEM((total, 8, 128), jnp.float32),
            dma((4,)),
            dma((2,)),
            dma((2,)),
            dma((3, n_out)),
            dma((n_out,)),
            dma((total,)),
            dma((total,)),
        ],
        compiler_params=pltpu.CompilerParams(
            collective_id=0, has_side_effects=True, vmem_limit_bytes=60 * 2**20),
        cost_estimate=pl.CostEstimate(
            flops=2 * queries * tokens * width * cols, bytes_accessed=2 * query_grads.size, transcendentals=0),
    )(activations, out_grads, query_grads)
    place = lax.rem(lax.axis_index(("outd", "ind")), 128 // share)
    return lax.dynamic_slice(sums, (0, place * share), (queries, share))


def plain(activations, out_grads, query_grads):
    gradient = lax.all_gather(out_grads, "ind", axis=0, tiled=True)
    gathered = lax.all_gather(activations, "outd", axis=0, tiled=True)
    projected = jnp.einsum("ti,qio->qto", gathered, query_grads, preferred_element_type=jnp.float32)
    partial_sum = jnp.einsum("qto,to->qt", projected, gradient.astype(jnp.float32))
    return lax.psum_scatter(partial_sum, ("outd", "ind"), scatter_dimension=1, tiled=True)


def local(n_out, n_in, activations, out_grads, query_grads):
    queries, width, cols = query_grads.shape
    block_t, half_t = activations.shape[0], out_grads.shape[0]
    tokens, total = block_t * n_out, n_out * n_in
    fits = (n_in == 2 and n_out == 4 * PLANE and queries <= 8 and queries % 2 == 0 and block_t % 16 == 0 and half_t % 128 == 0
            and cols % 128 == 0 and width % (2 * ROWS) == 0 and width // ROWS >= 8 and tokens % 128 == 0
            and 128 % (tokens // total) == 0
            and (3 * queries * ROWS * cols + tokens * (cols + width)) * 2 + queries * width * tokens * 4 < 56 * 2**20)
    if fits:
        return fused(n_out, n_in, activations, out_grads, query_grads)
    return plain(activations, out_grads, query_grads)


def solution(mesh):
    in_specs = (P(("groups", "outd"), "ind"), P(("groups", "ind"), "outd"), P(None, "ind", "outd"))
    out_specs = P(None, ("groups", "outd", "ind"))
    return jax.shard_map(functools.partial(local, mesh.shape["outd"], mesh.shape["ind"]),
                         mesh=mesh, in_specs=in_specs, out_specs=out_specs, check_vma=False)
```
